128 devices in a mesh: walk: 4 (over x), chol: 32 (over y, z, core).
Axes of the slice: x: 4, y: 4, z: 4, core: 2. Of those that a mesh axis runs over, the one named last changes fastest.
Arguments:
- walkers: bfloat16 [16, 640, 200], P('walk'), as said below
- trial: bfloat16 [640, 200], replicated
- half_chol: bfloat16 [1792, 640, 200], P('chol', 'walk'), may hold values from -0.3984375 to 0.3984375
- chol_vectors: bfloat16 [1792, 640, 640], P('chol', 'walk'), may hold values from -0.001953125 to 0.001953125
- noise: float32 [16, 1792], P('walk', 'chol'), may hold values from -6 to 6
- copies: int32 [16], replicated, may hold values from 0 to 12, as said below
Outputs:
- new_walkers: bfloat16 [16, 640, 200], P('walk')
- energies: float32 [16], P('walk')
The draws below stay inside these ranges and needn't reach their ends.
Inputs may be any that keep to these rules, and one draw needn't show every extreme that they name: copies sum to 16; exactly one walker, one of the first 4, has the most copies; every walker before it has one copy, every other walker one or none. trial^T walkers[w] is invertible for every walker.
All inputs are finite; a program needn't handle non-finite values.
Results may differ from the reference program's by a relative error of at most 0.0084.
Values may be sent and summed in bfloat16 or wider, within the bound.
No kernel may reach another device: no remote copies, remote signals or barrier semaphores. Data moves between devices by JAX's collectives and lax.ppermute only.
A program may use at most 256 MiB of HBM per device.

```python
import jax
import jax.numpy as jnp
from jax import lax

N = 640
NOCC = 200
CH_DEV = 56
W_GRP = 4
TERMS = 4
CHOL = 1792
WALKERS = 16


def orbital_block(key, spread):
    upper_key, lower_key, scale_key = jax.random.split(key, 3)
    upper = jnp.eye(NOCC, dtype=jnp.float32) + jax.random.normal(upper_key, (NOCC, NOCC), jnp.float32) * (0.3 / NOCC ** 0.5)
    lower = jax.random.normal(lower_key, (N - NOCC, NOCC), jnp.float32) * (0.5 / N ** 0.5)
    scales = jnp.exp(jax.random.uniform(scale_key, (N - NOCC, 1), jnp.float32, -spread, spread))
    return jnp.concatenate([upper, lower * scales], axis=0)


def mixed_block(key, spread):
    block_key, order_key, sign_key = jax.random.split(key, 3)
    block = orbital_block(block_key, spread)
    order = jax.random.permutation(order_key, NOCC).astype(jnp.int32)
    flips = jax.random.permutation(sign_key, NOCC).astype(jnp.int32)
    signs = jnp.where(flips < NOCC // 2, -1.0, 1.0).astype(jnp.float32)
    return block[:, order] * signs[None, :]


def draw_walkers(key, part):
    key = jax.random.fold_in(key, 11)
    keys = jax.random.split(key, WALKERS)
    spread = 0.0
    return jax.vmap(lambda k: mixed_block(k, spread))(keys).astype(jnp.bfloat16)


def draw_trial(key, part):
    key = jax.random.fold_in(key, 23)
    spread = 0.0
    return orbital_block(key, spread).astype(jnp.bfloat16)


def draw_copies(key, part):
    key = jax.random.fold_in(key, 37)
    first, second = jax.random.split(key)
    most = WALKERS // 2 + W_GRP
    rest = WALKERS - most
    hub = jax.random.randint(first, (), 0, W_GRP).astype(jnp.int32)
    places = jnp.arange(WALKERS, dtype=jnp.int32)
    shuffled = jax.random.permutation(second, WALKERS).astype(jnp.int32)
    scores = jnp.where(places > hub, shuffled, shuffled + WALKERS).astype(jnp.int32)
    order = jnp.argsort(scores, stable=True).astype(jnp.int32)
    ranks = jnp.argsort(order, stable=True).astype(jnp.int32)
    chosen = (ranks < rest - hub).astype(jnp.int32)
    before = (places < hub).astype(jnp.int32)
    return (chosen + before + most * (places == hub).astype(jnp.int32)).astype(jnp.int32)


def levels(rng, dims, cuts, low, top_value):
    def one(position, parts):
        steps = jax.random.uniform(jax.random.fold_in(jax.random.fold_in(rng, 6), position), (parts,), jnp.float32, low / len(cuts), top_value / len(cuts))
        return jnp.repeat(jnp.exp(steps), dims[position] // parts).reshape((-1,) + (1,) * (len(dims) - position - 1))

    level = one(*cuts[0])
    for cut in cuts[1:]:
        level = level * one(*cut)
    return level


def normal_values(key, shape, width, bound, cuts=(), kind=jnp.bfloat16):
    result = width * jax.random.normal(key, shape, jnp.float32)
    if cuts:
        result = result * levels(key, shape, cuts, -0.22, 0.18)
    return jnp.clip(result, -bound, bound).astype(kind)


def setup_inputs(seed: int = 0) -> dict:
    key_list = jax.random.split(jax.random.key(seed), 7)
    walkers = draw_walkers(jax.random.fold_in(key_list[6], 71), 0)
    trial = draw_trial(jax.random.fold_in(key_list[6], 71), 0)
    half_chol = normal_values(key_list[2], (CHOL, N, NOCC), 0.065, 0.3984375, ((0, 32), (1, 4)))
    chol_vectors = normal_values(key_list[3], (CHOL, N, N), (8 * N * CHOL) ** -0.5, 0.001953125, ((0, 32), (1, 4)))
    noise = normal_values(key_list[4], (WALKERS, CHOL), 1.0, 6.0, ((0, 4), (1, 32)), jnp.float32)
    copies = draw_copies(jax.random.fold_in(key_list[6], 71), 0)
    return dict(walkers=walkers, trial=trial, half_chol=half_chol, chol_vectors=chol_vectors, noise=noise, copies=copies)


def make_theta(walker, trial):
    wide = walker.astype(jnp.float32)
    correlation = jnp.dot(trial.astype(jnp.float32).T, wide, precision=lax.Precision.HIGHEST)
    gram = jnp.dot(correlation.T, correlation, precision=lax.Precision.HIGHEST)
    factor = jnp.linalg.cholesky(gram)
    inverse = jax.scipy.linalg.cho_solve((factor, True), correlation.T)
    return jnp.dot(wide, inverse, precision=lax.Precision.HIGHEST).astype(jnp.bfloat16)

def reference(walkers, trial, half_chol, chol_vectors, noise, copies):
    theta = jax.vmap(lambda w: make_theta(w, trial))(walkers)
    blocks = half_chol.reshape(CHOL // CH_DEV, CH_DEV, N, NOCC)

    def per_walker(one):
        wide = one.astype(jnp.float32)

        def per_block(block):
            pairs = jnp.einsum('gri,rj->gij', block.astype(jnp.float32), wide, precision=lax.Precision.HIGHEST)
            bias = jnp.einsum('gii->g', pairs)
            cross = jnp.einsum('gij,gji->g', pairs, pairs)
            return (bias, cross)
        bias, cross = lax.map(per_block, blocks)
        return (bias.reshape(CHOL), cross.reshape(CHOL))
    bias, cross = lax.map(per_walker, theta)
    field = (noise - 0.5 * bias).astype(jnp.bfloat16)
    chol_blocks = chol_vectors.reshape(CHOL // CH_DEV, CH_DEV, N * N)
    field_blocks = field.reshape(WALKERS, CHOL // CH_DEV, CH_DEV).transpose(1, 0, 2)

    def add_block(total, pair):
        fpart, lpart = pair
        return (total + jnp.dot(fpart.astype(jnp.float32), lpart.astype(jnp.float32), precision=lax.Precision.HIGHEST), None)
    potential, _ = lax.scan(add_block, jnp.zeros((WALKERS, N * N), jnp.float32), (field_blocks, chol_blocks))
    potential = potential.reshape(WALKERS, N, N).astype(jnp.bfloat16)
    term = walkers
    total = walkers.astype(jnp.float32)
    for k in range(1, TERMS + 1):
        term = (jnp.einsum('wrs,wsn->wrn', potential.astype(jnp.float32), term.astype(jnp.float32), precision=lax.Precision.HIGHEST) / k).astype(jnp.bfloat16)
        total = total + term.astype(jnp.float32)
    propagated = total.astype(jnp.bfloat16)
    energies = jnp.sum(0.5 * bias * bias - 0.5 * cross, axis=1) / CHOL
    ends = jnp.cumsum(copies).astype(jnp.int32)
    slots = jnp.arange(WALKERS, dtype=jnp.int32)
    parent = jnp.sum((ends[None, :] <= slots[:, None]).astype(jnp.int32), axis=1).astype(jnp.int32)
    new_walkers = propagated[parent]
    return (new_walkers, energies)
```

```python
import functools

import jax
import jax.numpy as jnp
from jax import lax
from jax.experimental import pallas as pl
from jax.experimental.pallas import tpu as pltpu
from jax.sharding import Mesh, PartitionSpec as P

TERMS = 4
BF = jnp.bfloat16
F32 = jnp.float32
HIGH = lax.Precision.HIGHEST
VMEM_LIMIT = 56 * 1024 * 1024
SMEM = pl.BlockSpec(memory_space=pltpu.SMEM)
VMEM = pl.BlockSpec(memory_space=pltpu.VMEM)


def params(**more):
    return pltpu.CompilerParams(vmem_limit_bytes=VMEM_LIMIT, **more)


def cost(flops, moved):
    return pl.CostEstimate(flops=int(flops), bytes_accessed=int(moved), transcendentals=0)


def mm(a, b, dims=((1,), (0,)), precision=None):
    return lax.dot_general(
        a, b, (dims, ((), ())), precision=precision, preferred_element_type=F32
    )


def shift(n, k):
    return [(q, (q + k) % n) for q in range(n)]


def theta_kernel(n, place, trial, walkers, *rest):
    own = rest[:n]
    others = rest[n : 2 * n - 1]
    c_ref, s_ref, x_ref = rest[2 * n - 1 :]
    x_at, core = place[0], place[3]
    pair = own[0].shape[0]
    rows = own[0].shape[1]
    n_occ = trial.shape[1]
    ids = [lax.broadcasted_iota(jnp.int32, (n_occ, n_occ), d) for d in (0, 1)]
    eye = (ids[0] == ids[1]).astype(F32)
    for i in range(pair):
        w = walkers[pair * core + i]
        c = mm(trial[...], w, ((0,), (0,)))
        ct = mm(w, trial[...], ((0,), (0,)))
        c_ref[i] = c
        g = jnp.abs(mm(c.astype(BF), ct.astype(BF)))
        side = jnp.max(jnp.sum(jnp.abs(c), axis=0)) * jnp.max(jnp.sum(jnp.abs(ct), axis=0))
        bound = jnp.max(jnp.sum(g, axis=0)) * 1.01 + side / 128.0
        start = ct * (1.9 / jnp.full(ct.shape, bound, F32))
        s_ref[i] = start
        x_ref[i] = start

    def coarse(state):
        step, _ = state
        xs = [x_ref[i] for i in range(pair)]
        rs = [eye - mm(c_ref[i].astype(BF), xs[i].astype(BF)) for i in range(pair)]
        for i in range(pair):
            x_ref[i] = xs[i] + mm(xs[i].astype(BF), rs[i].astype(BF))
        worst = sum(jnp.sum(r * r) for r in rs)
        return step + 1, worst

    def fine(state):
        step, _ = state
        xs = [x_ref[i] for i in range(pair)]
        rs = [eye - mm(c_ref[i], xs[i], precision=HIGH) for i in range(pair)]
        bs = [r.astype(BF) for r in rs]
        twos = [(rs[i] + mm(bs[i], bs[i])).astype(BF) for i in range(pair)]
        for i in range(pair):
            x_ref[i] = xs[i] + mm(xs[i].astype(BF), twos[i])
        worst = sum(jnp.sum(r * r) for r in rs)
        return step + 1, worst

    def far(limit, tolerance):
        return lambda state: (state[0] < limit) & jnp.logical_not(state[1] < tolerance)

    begin = (jnp.int32(0), jnp.float32(1e30))
    lax.while_loop(far(14, 0.3), coarse, begin)
    _, left = lax.while_loop(far(6, 0.005), fine, begin)

    @pl.when(jnp.logical_not(left < 0.005))
    def _():
        x_ref[...] = s_ref[...]
        lax.while_loop(far(60, 0.005), fine, begin)

    for i in range(pair):
        inv = x_ref[i]
        high = inv.astype(BF)
        low = (inv - high.astype(F32)).astype(BF)
        for j in range(n):
            block = lax.rem(x_at + j, n)
            w = walkers[pair * core + i, pl.ds(pl.multiple_of(block * rows, rows), rows), :]
            theta = (mm(w, high) + mm(w, low)).astype(BF)
            own[j][i] = theta
            for k in range(1, n):
                if j != k:
                    others[k - 1][j - (j > k), i] = theta


def make_theta(place, trial, walkers, n):
    _, n_orb, n_occ = walkers.shape
    rows = n_orb // n
    pair = walkers.shape[0] // 2
    small = jax.ShapeDtypeStruct((pair, rows, n_occ), BF)
    big = jax.ShapeDtypeStruct((n - 1, pair, rows, n_occ), BF)
    return pl.pallas_call(
        functools.partial(theta_kernel, n),
        out_shape=[small] * n + [big] * (n - 1),
        in_specs=[SMEM, VMEM, VMEM],
        out_specs=[VMEM] * (2 * n - 1),
        scratch_shapes=[pltpu.VMEM((pair, n_occ, n_occ), F32)] * 3,
        compiler_params=params(),
        cost_estimate=cost(1e10, 4e6),
        name="theta",
    )(place, trial, walkers)


def bias_kernel(n, place, half, noise, *rest):
    thetas = rest[: 2 * n]
    out, t_ref = rest[2 * n :]
    x_at, core = place[0], place[3]
    pair, rows, n_occ = thetas[0].shape
    lanes = 16
    walkers = 2 * n * pair
    chunks = rows // lanes
    step = pl.program_id(0)
    block = half.shape[0]
    n_vec = out.shape[1] // 2

    @pl.when(step == 0)
    def _():
        for l in range(walkers):
            t_ref[:, l * lanes : (l + 1) * lanes, :] = thetas[l // pair][l % pair].reshape(
                chunks, lanes, n_occ
            )
        out[...] = jnp.zeros(out.shape, F32)
        group = lax.broadcasted_iota(jnp.int32, (noise.shape[0], walkers), 0) + 2 * pair * x_at
        column = lax.broadcasted_iota(jnp.int32, (noise.shape[0], walkers), 1)
        out[1, pl.ds(pl.multiple_of(core * n_vec, 8), n_vec), :] = mm(
            noise[...], (group == column).astype(F32), ((0,), (0,)), HIGH
        )

    total = jnp.zeros((block * lanes, walkers * lanes), F32)
    for c in range(chunks):
        rows_c = half[:, c * lanes : (c + 1) * lanes, :].reshape(block * lanes, n_occ)
        total = total + mm(rows_c, t_ref[c], ((1,), (1,)))
    r0 = lax.broadcasted_iota(jnp.int32, total.shape, 0) % lanes
    r1 = lax.broadcasted_iota(jnp.int32, total.shape, 1) % lanes
    kept = jnp.where(r0 == r1, total, 0.0).reshape(block, lanes, walkers * lanes)
    per = jnp.sum(kept, axis=1)
    lane = lax.broadcasted_iota(jnp.int32, (walkers * lanes, walkers), 0) // lanes
    source = lane // pair
    k = source % n
    c = jnp.where(source < n, core, 1 - core)
    walker = 2 * pair * ((x_at - k + n) % n) + pair * c + lane % pair
    column = lax.broadcasted_iota(jnp.int32, (walkers * lanes, walkers), 1)
    picked = mm(per, (walker == column).astype(F32), precision=HIGH)
    out[0, pl.ds(pl.multiple_of(core * n_vec + step * block, 8), block), :] = picked


def make_bias(place, half, noise, thetas, n):
    n_vec, rows, n_occ = half.shape
    pair = thetas[0].shape[0]
    walkers = 2 * n * pair
    block = 8
    return pl.pallas_call(
        functools.partial(bias_kernel, n),
        out_shape=jax.ShapeDtypeStruct((2, 2 * n_vec, walkers), F32),
        grid=(n_vec // block,),
        in_specs=[SMEM, pl.BlockSpec((block, rows, n_occ), lambda s: (s, 0, 0)), VMEM]
        + [VMEM] * (2 * n),
        out_specs=VMEM,
        scratch_shapes=[pltpu.VMEM((rows // 16, walkers * 16, n_occ), BF)],
        compiler_params=params(),
        cost_estimate=cost(4e9, 8e6),
        name="bias",
    )(place, half, noise, *thetas)


def potential_kernel(n, place, summed, picker, mine, theirs, *rest):
    outs = rest[:n]
    (a_ref,) = rest[n:]
    core = place[3]
    n_vec, lanes, n_orb = mine.shape
    slots = picker.shape[0]

    @pl.when(pl.program_id(0) == 0)
    def _():
        field = (summed[1] - 0.5 * summed[0]).astype(BF)
        chosen = mm(picker[...], field, ((1,), (1,))).astype(BF)
        vec = lax.broadcasted_iota(jnp.int32, (n_vec, n_vec * lanes), 0)
        lane = lax.broadcasted_iota(jnp.int32, (n_vec, n_vec * lanes), 1)
        spread = (lane // lanes == vec).astype(F32).astype(BF)
        sub = lax.broadcasted_iota(jnp.int32, (lanes, n_vec * lanes), 0)
        along = lax.broadcasted_iota(jnp.int32, (lanes, n_vec * lanes), 1) % lanes
        same = (sub == along).astype(F32)
        for c in range(2):
            wide = mm(chosen[:, c * n_vec : (c + 1) * n_vec], spread)
            for s in range(slots):
                a_ref[c, s * lanes : (s + 1) * lanes, :] = (same * wide[s : s + 1, :]).astype(BF)

    got = mm(a_ref[core], mine[...].reshape(n_vec * lanes, n_orb)) + mm(
        a_ref[1 - core], theirs[...].reshape(n_vec * lanes, n_orb)
    )
    got = got.astype(BF).reshape(slots, lanes, n_orb)
    each = slots // n
    for k in range(n):
        outs[k][...] = got[k * each : (k + 1) * each]


def make_potential(place, summed, picker, mine, theirs, n):
    n_vec, rows, n_orb = mine.shape
    slots = picker.shape[0]
    half = rows // 2
    lanes = 16
    steps = half // lanes
    rows_of = pl.BlockSpec((n_vec, lanes, n_orb), lambda s, p: (0, p[3] * steps + s, 0))
    whole = pl.BlockSpec(memory_space=pltpu.VMEM)
    return pl.pallas_call(
        functools.partial(potential_kernel, n),
        out_shape=[jax.ShapeDtypeStruct((slots // n, half, n_orb), BF)] * n,
        grid_spec=pltpu.PrefetchScalarGridSpec(
            num_scalar_prefetch=1,
            grid=(steps,),
            in_specs=[whole, whole, rows_of, rows_of],
            out_specs=[pl.BlockSpec((slots // n, lanes, n_orb), lambda s, p: (0, s, 0))] * n,
            scratch_shapes=[pltpu.VMEM((2, slots * lanes, n_vec * lanes), BF)],
        ),
        compiler_params=params(),
        cost_estimate=cost(4e9, 1.5e7),
        name="potential",
    )(place, summed, picker, mine, theirs)


def cross_kernel(n, pieces, place, *rest):
    k = pieces[0]
    halves = rest[: 2 * n]
    n_theta = len(pieces[1])
    thetas = rest[2 * n : 2 * n + n_theta]
    out, h_ref, t_ref, acc = rest[2 * n + n_theta :]
    x_at = place[0]
    rows, n_occ = halves[0].shape[1:]
    pair = acc.shape[0]
    step = pl.program_id(0)

    def at(block):
        return pl.ds(pl.multiple_of(lax.rem(block, n) * rows, rows), rows)

    @pl.when(step == 0)
    def _():
        acc[...] = jnp.zeros(acc.shape, F32)
        for i in range(pair):
            for ref, part in zip(thetas, pieces[1]):
                for place_in, j in part:
                    block = ref[i] if place_in is None else ref[place_in, i]
                    h_ref[at(x_at - k + n + j), :] = block
            t_ref[i * n_occ : (i + 1) * n_occ, :] = h_ref[...].astype(F32).T.astype(BF)

    for side in range(2):
        for s in range(n):
            h_ref[at(x_at - s + n), :] = halves[side * n + s][0]
        got = mm(t_ref[...], h_ref[...])
        for i in range(pair):
            p = got[i * n_occ : (i + 1) * n_occ].astype(BF)
            acc[i] += mm(p, p)

    @pl.when(step == pl.num_programs(0) - 1)
    def _():
        ids = [lax.broadcasted_iota(jnp.int32, (n_occ, n_occ), d) for d in (0, 1)]
        for i in range(pair):
            out[i] = jnp.full(out.shape[1:], jnp.sum(jnp.where(ids[0] == ids[1], acc[i], 0.0)), F32)


def make_cross(k, place, halves, thetas, part, n):
    count, rows, n_occ = halves[0].shape
    pair = 2
    return pl.pallas_call(
        functools.partial(cross_kernel, n, (k, part)),
        out_shape=jax.ShapeDtypeStruct((pair, 8, 128), F32),
        grid=(count,),
        in_specs=[SMEM]
        + [pl.BlockSpec((1, rows, n_occ), lambda s: (s, 0, 0))] * (2 * n)
        + [VMEM] * len(thetas),
        out_specs=VMEM,
        scratch_shapes=[
            pltpu.VMEM((n * rows, n_occ), BF),
            pltpu.VMEM((pair * n_occ, n * rows), BF),
            pltpu.VMEM((pair, n_occ, n_occ), F32),
        ],
        compiler_params=params(),
        cost_estimate=cost(7e9, 1.2e7),
        name="cross",
    )(place, *halves, *thetas)


def taylor_kernel(n, place, walker, *rest):
    parts = rest[: 2 * n]
    mine, other, v_ref = rest[2 * n :]
    z_at, core = place[2], place[3]
    half = parts[0].shape[0]
    for k in range(n):
        block = lax.rem(z_at - k + n, n)
        v_ref[pl.ds(pl.multiple_of((2 * block + core) * half, half), half), :] = parts[k][...]
        v_ref[pl.ds(pl.multiple_of((2 * block + 1 - core) * half, half), half), :] = parts[n + k][...]
    term = walker[...]
    total = term.astype(F32)
    for k in range(1, TERMS + 1):
        term = (mm(v_ref[...], term) / k).astype(BF)
        total = total + term.astype(F32)
    done = total.astype(BF)
    rows = done.shape[0] // 2
    first = core == 0
    mine[...] = jnp.where(first, done[:rows].astype(F32), done[rows:].astype(F32)).astype(BF)
    other[...] = jnp.where(first, done[rows:].astype(F32), done[:rows].astype(F32)).astype(BF)


def make_taylor(place, walker, parts, n):
    n_orb, n_occ = walker.shape
    half = jax.ShapeDtypeStruct((n_orb // 2, n_occ), BF)
    return pl.pallas_call(
        functools.partial(taylor_kernel, n),
        out_shape=[half, half],
        in_specs=[SMEM] + [VMEM] * (1 + 2 * n),
        out_specs=[VMEM] * 2,
        scratch_shapes=[pltpu.VMEM((n_orb, n_orb), BF)],
        compiler_params=params(),
        cost_estimate=cost(1.3e9, 2e6),
        name="taylor",
    )(place, walker, *parts)


def join_kernel(n, place, *rest):
    parts, out = rest[:-1], rest[-1]
    y_at, core = place[1], place[3]
    rows = parts[0].shape[0]
    for k in range(n):
        slot = lax.rem(y_at - k + n, n)
        out[slot, pl.ds(pl.multiple_of(core * rows, rows), rows), :] = parts[k][...]
        out[slot, pl.ds(pl.multiple_of((1 - core) * rows, rows), rows), :] = parts[n + k][...]


def join(place, parts, n):
    rows, n_occ = parts[0].shape
    return pl.pallas_call(
        functools.partial(join_kernel, n),
        out_shape=jax.ShapeDtypeStruct((n, 2 * rows, n_occ), BF),
        in_specs=[SMEM] + [VMEM] * (2 * n),
        out_specs=VMEM,
        compiler_params=params(),
        cost_estimate=cost(1e6, 2e6),
        name="join",
    )(place, *parts)


def shards(walkers, trial, half_chol, chol_vectors, noise, copies):
    n = lax.axis_size("x")
    x, y, z, core = (lax.axis_index(a) for a in ("x", "y", "z", "core"))
    place = jnp.stack([x, y, z, core]).astype(jnp.int32)
    w_grp, n_orb, n_occ = walkers.shape
    n_vec = half_chol.shape[0]
    slots = w_grp * n
    other_core = functools.partial(lax.ppermute, axis_name="core", perm=[(0, 1), (1, 0)])

    def along(v, axis, k):
        return lax.ppermute(v, axis, shift(n, k)) if k else v

    parent = jnp.sum(
        (jnp.cumsum(copies)[None, :] <= jnp.arange(slots, dtype=jnp.int32)[:, None]).astype(jnp.int32),
        axis=1,
    )

    per = n_vec // n
    halves = [
        along(lax.dynamic_slice_in_dim(half_chol, (x + k) % n * per, per, 0), "x", k) for k in range(n)
    ]
    halves = halves + [other_core(h) for h in halves]
    chol_theirs = other_core(chol_vectors)

    def offered(k):
        wanted = parent[(x + k) % n * w_grp + y] - w_grp * x
        return along(
            lax.dynamic_index_in_dim(walkers, jnp.clip(wanted, 0, w_grp - 1), 0, keepdims=False), "x", k
        )

    home = parent[x * w_grp + y] // w_grp
    offers = [offered(k) for k in range(n)]
    walker = offers[0]
    for k in range(1, n):
        walker = jnp.where((x - k) % n == home, offers[k], walker)

    made = make_theta(place, trial, walkers, n)
    own, rest = made[:n], made[n:]
    rows_here = [along(own[k], "x", k) for k in range(n)]
    thetas = rows_here + [other_core(t) for t in rows_here]
    partial_bias = make_bias(place, half_chol, noise, thetas, n)
    summed = lax.psum(partial_bias, ("x", "core"))

    order = jnp.array([[k, m] for k in range(n) for m in range(n)], jnp.int32)
    slot = w_grp * ((z + order[:, 1]) % n) + (y + order[:, 0]) % n
    picker = (parent[slot][:, None] == jnp.arange(slots, dtype=jnp.int32)[None, :]).astype(BF)
    partials = make_potential(place, summed, picker, chol_vectors, chol_theirs, n)

    def added(parts):
        total = parts[0].astype(F32)
        for p in parts[1:]:
            total = total + p.astype(F32)
        return total.astype(BF)

    over_y = added([along(partials[k], "y", k) for k in range(n)])
    piece = added([along(over_y[m], "z", m) for m in range(n)])
    cross_plane = [
        lax.ppermute(
            piece, ("x", "z"), [(n * a + b, n * b + (a + k) % n) for a in range(n) for b in range(n)]
        )
        for k in range(n)
    ]
    parts = cross_plane + [other_core(p) for p in cross_plane]
    mine, other = make_taylor(place, walker, parts, n)
    spread = [along(mine, "y", k) for k in range(n)]
    new_walkers = join(place, spread + [other] + [other_core(s) for s in spread[1:]], n)

    crosses = []
    for k in range(n):
        if k == 0:
            arrays, part = own, [[(None, j)] for j in range(n)]
        else:
            arrays = [rows_here[k], along(rest[k - 1], "x", k)]
            part = [[(None, k)], [(j - (j > k), j) for j in range(n) if j != k]]
        crosses.append(make_cross(k, place, halves, arrays, part, n))
    local = 0.5 / (2 * n) * jnp.sum(summed[0] * summed[0], axis=0)
    for k in range(n):
        first = w_grp * ((x - k) % n) + 2 * core
        local = lax.dynamic_update_slice(
            local, lax.dynamic_slice(local, (first,), (2,)) - 0.5 * crosses[k][:, 0, 0], (first,)
        )
    every = lax.all_gather(local.reshape(1, slots), ("x", "y", "z", "core"), axis=0, tiled=True)
    n_all = n_vec * 2 * n * n
    energies = lax.dynamic_slice_in_dim(jnp.sum(every, axis=0), w_grp * x, w_grp) / n_all
    return new_walkers, energies


def solution(mesh):
    finer = Mesh(mesh.devices.reshape(4, 4, 4, 2), ("x", "y", "z", "core"))
    chol = ("y", "z", "core")
    placed = (
        P("x", None, None),
        P(),
        P(chol, "x", None),
        P(chol, "x", None),
        P("x", chol),
        P(),
    )
    return jax.shard_map(
        shards,
        mesh=finer,
        in_specs=placed,
        out_specs=(P("x", None, None), P("x")),
        check_vma=False,
    )
```

```python
import functools

import jax
import jax.numpy as jnp
from jax import lax
from jax.experimental import pallas as pl
from jax.experimental.pallas import tpu as pltpu
from jax.sharding import Mesh, PartitionSpec as P

TERMS = 4
BF = jnp.bfloat16
F32 = jnp.float32
HIGH = lax.Precision.HIGHEST
VMEM_LIMIT = 56 * 1024 * 1024
SMEM = pl.BlockSpec(memory_space=pltpu.SMEM)
VMEM = pl.BlockSpec(memory_space=pltpu.VMEM)


def params(**more):
    return pltpu.CompilerParams(vmem_limit_bytes=VMEM_LIMIT, **more)


def taking(us):
    return pl.CostEstimate(flops=int(us * 1.15e9), bytes_accessed=1, transcendentals=0)


def mm(a, b, dims=((1,), (0,)), precision=None):
    return lax.dot_general(
        a, b, (dims, ((), ())), precision=precision, preferred_element_type=F32
    )


def shift(n, k):
    return [(q, (q + k) % n) for q in range(n)]


def theta_kernel(n, quarter, place, wanted, trial, walkers, *rest):
    own, (sent, c_ref, s_ref, y_ref, w_ref, h_ref, whole) = rest[:n], rest[n:]
    x_at, z_at, core = place[0], place[2], place[3]
    pair, rows = own[0].shape[:2]
    n_occ = trial.shape[0]
    ids = [lax.broadcasted_iota(jnp.int32, (n_occ, n_occ), d) for d in (0, 1)]
    eye = (ids[0] == ids[1]).astype(F32)
    for i in range(pair):
        w = walkers[pair * core + i]
        c = mm(trial[...], w, ((1,), (1,)))
        ct = mm(w, trial[...], ((1,), (1,)))
        c_ref[i] = ct
        g = jnp.abs(mm(c.astype(BF), ct.astype(BF)))
        side = jnp.max(jnp.sum(jnp.abs(c), axis=0)) * jnp.max(jnp.sum(jnp.abs(ct), axis=0))
        bound = jnp.max(jnp.sum(g, axis=0)) * 1.01 + side / 128.0
        start = c * (1.9 / jnp.full(ct.shape, bound, F32))
        s_ref[i] = start
        y_ref[i] = start

    def coarse(state):
        step, _ = state
        ys = [y_ref[i] for i in range(pair)]
        rs = [eye - mm(c_ref[i].astype(BF), ys[i].astype(BF)) for i in range(pair)]
        for i in range(pair):
            y_ref[i] = ys[i] + mm(ys[i].astype(BF), rs[i].astype(BF))
        return step + 1, sum(jnp.sum(r * r) for r in rs)

    def fine(state):
        step, _ = state
        ys = [y_ref[i] for i in range(pair)]
        rs = [eye - mm(c_ref[i], ys[i], precision=HIGH) for i in range(pair)]
        bs = [r.astype(BF) for r in rs]
        twos = [(rs[i] + mm(bs[i], bs[i])).astype(BF) for i in range(pair)]
        for i in range(pair):
            y_ref[i] = ys[i] + mm(ys[i].astype(BF), twos[i])
        return step + 1, sum(jnp.sum(r * r) for r in rs)

    def far(limit, tolerance):
        return lambda state: (state[0] < limit) & jnp.logical_not(state[1] < tolerance)

    begin = (jnp.int32(0), jnp.float32(1e30))
    lax.while_loop(far(14, 0.3), coarse, begin)
    _, left = lax.while_loop(far(6, 0.005), fine, begin)

    @pl.when(jnp.logical_not(left < 0.005))
    def _():
        y_ref[...] = s_ref[...]
        lax.while_loop(far(60, 0.005), fine, begin)

    for i in range(pair):
        inv = y_ref[i]
        high = inv.astype(BF)
        low = (inv - high.astype(F32)).astype(BF)
        w = walkers[pair * core + i]
        turned = mm(high, w) + mm(low, w)
        w_ref[i * n_occ : (i + 1) * n_occ, :] = turned
        h_ref[...] = turned.T.astype(BF)
        for j in range(n):
            block = lax.rem(x_at + j, n)
            own[j][i] = h_ref[pl.ds(pl.multiple_of(block * rows, rows), rows), :]
    whole[...] = w_ref[...].astype(BF)
    stride = (whole.shape[0] - quarter) // (n - 1)
    count = sent.shape[1] - quarter
    far = n_occ - count
    for j in range(n):
        sent[j, :quarter, :] = whole[pl.ds(pl.multiple_of(z_at * stride, stride), quarter), :]
        sent[j, quarter:, :] = walkers[wanted[j], pl.ds(pl.multiple_of(core * far, far), count), :]


def make_theta(place, wanted, trial, walkers, n, quarter, count):
    _, n_occ, n_orb = walkers.shape
    pair = walkers.shape[0] // 2
    return pl.pallas_call(
        functools.partial(theta_kernel, n, quarter),
        out_shape=[jax.ShapeDtypeStruct((pair, n_orb // n, n_occ), BF)] * n
        + [
            jax.ShapeDtypeStruct((n, quarter + count, n_orb), BF),
        ],
        in_specs=[SMEM, SMEM, VMEM, VMEM],
        out_specs=[VMEM] * (n + 1),
        scratch_shapes=[pltpu.VMEM((pair, n_occ, n_occ), F32)] * 3
        + [
            pltpu.VMEM((pair * n_occ, n_orb), F32),
            pltpu.VMEM((n_orb, n_occ), BF),
            pltpu.VMEM((pair * n_occ, n_orb), BF),
        ],
        compiler_params=params(),
        cost_estimate=taking(7.6),
        name="theta",
    )(place, wanted, trial, walkers)


def bias_kernel(n, place, mine, theirs, noise_mine, noise_theirs, *rest):
    thetas, (out, t_ref, acc) = rest[:n], rest[n:]
    x_at, core = place[0], place[3]
    pair, rows, n_occ = thetas[0].shape
    lanes = 32
    chunks = rows // lanes
    block = mine.shape[0]
    n_vec = acc.shape[1]
    walkers = out.shape[0]
    width = n * pair * lanes
    step = pl.program_id(0)
    sub = 8

    @pl.when(step == 0)
    def _():
        for k in range(n):
            for i in range(pair):
                at = (k * pair + i) * lanes
                t_ref[:, at : at + lanes, :] = thetas[k][i].reshape(chunks, lanes, n_occ)

    along = lax.broadcasted_iota(jnp.int32, (1, lanes // sub, sub, width), 3) % lanes
    row = sub * lax.broadcasted_iota(jnp.int32, along.shape, 1) + lax.broadcasted_iota(
        jnp.int32, along.shape, 2
    )
    for side, ref in enumerate((mine, theirs)):
        got = jnp.zeros((block * lanes, width), F32)
        for c in range(chunks):
            left = ref[:, c * lanes : (c + 1) * lanes, :].reshape(block * lanes, n_occ)
            got = got + mm(left, t_ref[c], ((1,), (1,)))
        got = got.reshape(block, lanes // sub, sub, width)
        kept = jnp.sum(jnp.where(along == row, got, 0.0), axis=1)
        acc[core if side == 0 else 1 - core, pl.ds(step * block, block)] = kept

    @pl.when(step == pl.num_programs(0) - 1)
    def _():
        lane = lax.broadcasted_iota(jnp.int32, (width, walkers), 0) // lanes
        column = lax.broadcasted_iota(jnp.int32, (width, walkers), 1)
        spot = pair * ((x_at - lane // pair + n) % n) + lane % pair
        sums = jnp.sum(acc[...].reshape(2 * n_vec, sub, width), axis=1)
        out[...] = -0.5 * mm((spot == column).astype(F32), sums, ((0,), (1,)), HIGH)
        own = pair_noise(place, noise_mine, noise_theirs, pair)
        row = lax.broadcasted_iota(jnp.int32, (walkers, pair), 0)
        which = lax.broadcasted_iota(jnp.int32, (walkers, pair), 1) + pair * x_at
        out[...] += mm((row == which).astype(F32), own, precision=HIGH)


def pair_noise(place, mine, theirs, pair):
    core = place[3]
    count, n_vec = mine.shape
    walker = lax.broadcasted_iota(jnp.int32, (pair, count), 1) - pair * core
    pick = (walker == lax.broadcasted_iota(jnp.int32, (pair, count), 0)).astype(F32)
    vec = lax.broadcasted_iota(jnp.int32, (n_vec, 2 * n_vec), 0)
    spot = lax.broadcasted_iota(jnp.int32, (n_vec, 2 * n_vec), 1)
    near = mm(mine[...], (vec + core * n_vec == spot).astype(F32), precision=HIGH)
    far = mm(theirs[...], (vec + (1 - core) * n_vec == spot).astype(F32), precision=HIGH)
    return mm(pick, near + far, precision=HIGH)


def make_bias(place, mine, theirs, noise_mine, noise_theirs, thetas, n):
    n_vec, rows, n_occ = mine.shape
    pair = thetas[0].shape[0]
    walkers = n * pair
    lanes = 32
    block = 14
    return pl.pallas_call(
        functools.partial(bias_kernel, n),
        out_shape=jax.ShapeDtypeStruct((walkers, 2 * n_vec), F32),
        grid=(n_vec // block,),
        in_specs=[SMEM]
        + [pl.BlockSpec((block, rows, n_occ), lambda s: (s, 0, 0))] * 2
        + [VMEM] * (2 + n),
        out_specs=VMEM,
        scratch_shapes=[
            pltpu.VMEM((rows // lanes, n * pair * lanes, n_occ), BF),
            pltpu.VMEM((2, n_vec, 8, n * pair * lanes), F32),
        ],
        compiler_params=params(),
        cost_estimate=taking(0.01),
        name="bias",
    )(place, mine, theirs, noise_mine, noise_theirs, *thetas)


def potential_kernel(n, place, near, far, noise_mine, noise_theirs, pick_near, pick_far, mine, theirs, *rest):
    outs = rest[:n]
    squares, a_ref = rest[n:]
    core = place[3]
    n_vec, lanes, n_orb = mine.shape
    x_at = place[0]
    slots = pick_near.shape[0]

    @pl.when(pl.program_id(0) == 0)
    def _():
        chosen = (
            mm(pick_near[...], near[...].astype(BF)) + mm(pick_far[...], far[...].astype(BF))
        ).astype(BF)
        pair = near.shape[0] // n
        row = lax.broadcasted_iota(jnp.int32, (pair, n * pair), 0) + pair * x_at
        which = lax.broadcasted_iota(jnp.int32, (pair, n * pair), 1)
        field = mm((row == which).astype(F32), near[...], precision=HIGH)
        bias = 2.0 * (pair_noise(place, noise_mine, noise_theirs, pair) - field)
        total = jnp.sum(bias * bias, axis=1, keepdims=True)
        lane = lax.broadcasted_iota(jnp.int32, (pair, slots), 1)
        walker = 2 * pair * x_at + pair * core + lax.broadcasted_iota(jnp.int32, (pair, slots), 0)
        spread = jnp.sum(jnp.where(lane == walker, 0.5 * total, 0.0), axis=0, keepdims=True)
        squares[...] = jnp.broadcast_to(spread, squares.shape)
        vec = lax.broadcasted_iota(jnp.int32, (n_vec, n_vec * lanes), 0)
        lane = lax.broadcasted_iota(jnp.int32, (n_vec, n_vec * lanes), 1)
        repeat = (lane // lanes == vec).astype(F32).astype(BF)
        sub = lax.broadcasted_iota(jnp.int32, (lanes, n_vec * lanes), 0)
        along = lax.broadcasted_iota(jnp.int32, (lanes, n_vec * lanes), 1) % lanes
        same = (sub == along).astype(F32)
        for c in range(2):
            wide = mm(chosen[:, c * n_vec : (c + 1) * n_vec], repeat)
            for s in range(slots):
                a_ref[c, s * lanes : (s + 1) * lanes, :] = (same * wide[s : s + 1, :]).astype(BF)

    got = mm(a_ref[core], mine[...].reshape(n_vec * lanes, n_orb)) + mm(
        a_ref[1 - core], theirs[...].reshape(n_vec * lanes, n_orb)
    )
    got = got.astype(BF).reshape(slots, lanes, n_orb)
    each = slots // n
    for k in range(n):
        outs[k][...] = got[k * each : (k + 1) * each]


def make_potential(place, small, mine, theirs, n):
    n_vec, rows, n_orb = mine.shape
    slots = small[-1].shape[0]
    half = rows // 2
    lanes = 16
    steps = half // lanes
    rows_of = pl.BlockSpec((n_vec, lanes, n_orb), lambda s, p: (0, p[3] * steps + s, 0))
    return pl.pallas_call(
        functools.partial(potential_kernel, n),
        out_shape=[jax.ShapeDtypeStruct((slots // n, half, n_orb), BF)] * n
        + [jax.ShapeDtypeStruct((8, slots), F32)],
        grid_spec=pltpu.PrefetchScalarGridSpec(
            num_scalar_prefetch=1,
            grid=(steps,),
            in_specs=[VMEM] * len(small) + [rows_of, rows_of],
            out_specs=[pl.BlockSpec((slots // n, lanes, n_orb), lambda s, p: (0, s, 0))] * n + [VMEM],
            scratch_shapes=[pltpu.VMEM((2, slots * lanes, n_vec * lanes), BF)],
        ),
        compiler_params=params(),
        cost_estimate=taking(0.01),
        name="potential",
    )(place, *small, mine, theirs)


def cross_kernel(n, pair, place, before, *rest):
    mine, theirs, halves = rest[:n], rest[n : 2 * n], rest[2 * n]
    out, t_ref, h_ref, p_ref, acc = rest[2 * n + 1 :]
    rows, n_occ = halves.shape[2:]
    z_at, core = place[2], place[3]
    block, count = pair * n_occ, mine[0].shape[1]
    stride = (block - count) // (n - 1)
    walkers = 2 * n * pair
    step = pl.program_id(0)

    @pl.when(step == 0)
    def _():
        acc[...] = jnp.zeros(acc.shape, F32)
        p_ref[...] = jnp.zeros(p_ref.shape, BF)
        for c, tables in enumerate((mine, theirs)):
            for j in range(n):
                start = stride * lax.rem(z_at - j + n, n)
                for k in range(n):
                    at = pl.multiple_of((c * n + k) * block + start, 16)
                    t_ref[pl.ds(at, count), :] = tables[j][k]

    def square():
        for w in range(walkers):
            p = p_ref[w]
            acc[w] += mm(p, p)

    for s in range(n):
        h_ref[s * rows : (s + 1) * rows, :] = halves[s, 0]
    square()
    for q in range(2 * n):
        got = mm(t_ref[q * block : (q + 1) * block, :], h_ref[...])
        for i in range(pair):
            p_ref[q * pair + i] = got[i * n_occ : (i + 1) * n_occ].astype(BF)

    @pl.when(step == pl.num_programs(0) - 1)
    def _():
        square()
        ids = [lax.broadcasted_iota(jnp.int32, (n_occ, n_occ), d) for d in (0, 1)]
        lane = lax.broadcasted_iota(jnp.int32, out.shape, 1)
        total = before[...]
        for c in range(2):
            for k in range(n):
                for i in range(pair):
                    got = acc[(c * n + k) * pair + i]
                    value = jnp.sum(jnp.where(ids[0] == ids[1], got, 0.0))
                    parity = core if c == 0 else 1 - core
                    walker = 2 * pair * k + pair * parity + i
                    total = total + jnp.where(lane == walker, -0.5 * value, 0.0)
        out[...] = total


def make_cross(place, before, tables, halves, n):
    _, steps, rows, n_occ = halves.shape
    n_orb = tables[0].shape[2]
    pair = 2
    walkers = 2 * n * pair
    return pl.pallas_call(
        functools.partial(cross_kernel, n, pair),
        out_shape=jax.ShapeDtypeStruct(before.shape, F32),
        grid=(steps,),
        in_specs=[SMEM]
        + [VMEM] * (2 * n + 1)
        + [pl.BlockSpec((n, 1, rows, n_occ), lambda s: (0, s, 0, 0))],
        out_specs=VMEM,
        scratch_shapes=[
            pltpu.VMEM((walkers * n_occ, n_orb), BF),
            pltpu.VMEM((n_orb, n_occ), BF),
            pltpu.VMEM((walkers, n_occ, n_occ), BF),
            pltpu.VMEM((walkers, n_occ, n_occ), F32),
        ],
        compiler_params=params(),
        cost_estimate=taking(0.5),
        name="cross",
    )(place, before, *tables, halves)


def taylor_kernel(n, place, chosen, walker, mine, theirs, out, v_ref):
    x_at, z_at, core = place[0], place[2], place[3]
    half = mine.shape[1]
    for k in range(n):
        block = lax.rem(z_at - k - x_at + 2 * n, n)
        v_ref[pl.ds(pl.multiple_of((2 * block + core) * half, half), half), :] = mine[k]
        v_ref[pl.ds(pl.multiple_of((2 * block + 1 - core) * half, half), half), :] = theirs[k]

    term = walker[0, walker.shape[1] - out.shape[0] :, :]
    total = term.astype(F32)
    for k in range(1, TERMS + 1):
        term = (mm(term, v_ref[...], ((1,), (1,))) / k).astype(BF)
        total = total + term.astype(F32)
    out[...] = total.astype(BF)


def make_taylor(place, chosen, walkers, mine, theirs, n, count):
    _, rows, n_orb = walkers.shape
    return pl.pallas_call(
        functools.partial(taylor_kernel, n),
        out_shape=jax.ShapeDtypeStruct((count, n_orb), BF),
        grid_spec=pltpu.PrefetchScalarGridSpec(
            num_scalar_prefetch=2,
            grid=(1,),
            in_specs=[pl.BlockSpec((1, rows, n_orb), lambda s, p, c: (c[0], 0, 0)), VMEM, VMEM],
            out_specs=VMEM,
            scratch_shapes=[pltpu.VMEM((n_orb, n_orb), BF)],
        ),
        compiler_params=params(),
        cost_estimate=taking(0.01),
        name="taylor",
    )(place, chosen, walkers, mine, theirs)


def join_kernel(n, place, mine, theirs, out):
    y_at, core = place[1], place[3]
    count = mine.shape[1]
    far = out.shape[1] - count
    for k in range(n):
        slot = lax.rem(y_at - k + n, n)
        out[slot, pl.ds(pl.multiple_of(core * far, far), count), :] = mine[k]
        out[slot, pl.ds(pl.multiple_of((1 - core) * far, far), count), :] = theirs[k]


def join(place, mine, theirs, n, n_occ):
    n_orb = mine.shape[2]
    return pl.pallas_call(
        functools.partial(join_kernel, n),
        out_shape=jax.ShapeDtypeStruct((n, n_occ, n_orb), BF),
        in_specs=[SMEM, VMEM, VMEM],
        out_specs=VMEM,
        compiler_params=params(),
        cost_estimate=taking(0.01),
        name="join",
    )(place, mine, theirs)


def after(value, *earlier):
    return lax.optimization_barrier((value, *earlier))[0]


def shards(walkers, trial, half_chol, chol_vectors, noise, copies):
    n = lax.axis_size("x")
    x, y, z, core = (lax.axis_index(a) for a in ("x", "y", "z", "core"))
    place = jnp.stack([x, y, z, core]).astype(jnp.int32)
    w_grp, n_orb, n_occ = walkers.shape
    n_vec = half_chol.shape[0]
    slots = w_grp * n
    walkers = walkers.transpose(0, 2, 1)
    trial = trial.T
    other_core = functools.partial(lax.ppermute, axis_name="core", perm=[(0, 1), (1, 0)])

    def along(v, axis, k):
        return lax.ppermute(v, axis, shift(n, k)) if k else v

    parent = jnp.sum(
        (jnp.cumsum(copies)[None, :] <= jnp.arange(slots, dtype=jnp.int32)[:, None]).astype(jnp.int32),
        axis=1,
    )

    noise_theirs = other_core(noise)
    half_theirs = other_core(half_chol)
    quarter, count = 112, 104
    wanted = jnp.clip(parent.reshape(n, w_grp)[:, y] - w_grp * x, 0, w_grp - 1)
    *own, sent = make_theta(place, wanted, trial, walkers, n, quarter, count)
    own = [own[0]] + [after(t, half_theirs, noise_theirs) for t in own[1:]]
    thetas = [along(own[k], "x", k) for k in range(n)]
    got = lax.all_to_all(after(sent, *thetas[1:]), "x", 0, 0, tiled=True)
    chol_theirs = other_core(after(chol_vectors, own[0], half_theirs, noise_theirs))

    share = make_bias(place, half_chol, half_theirs, noise, noise_theirs, thetas, n)
    near = lax.psum(share, "x")
    got = after(got, near)
    distant = other_core(near)
    by_x = half_chol.reshape((n, n_vec // n) + half_chol.shape[1:])
    halves = lax.all_to_all(after(by_x, near), "x", 0, 0, tiled=True)

    pieces = got[:, :quarter]
    after_one, before_one = along(pieces, "z", 1), along(pieces, "z", 3)
    opposite = jnp.concatenate(
        [along(after_one[: n // 2], "z", 1), along(before_one[n // 2 :], "z", 3)], axis=0
    )
    tables = [pieces, after_one, opposite, before_one]
    order = jnp.array([[k, m] for k in range(n) for m in range(n)], jnp.int32)
    slot = w_grp * ((z + order[:, 1] - x) % n) + (y + order[:, 0]) % n
    pairs = jnp.array([w_grp * a + i for a in range(n) for i in range(w_grp // 2)], jnp.int32)
    pick_near, pick_far = [
        (parent[slot][:, None] == (pairs + w_grp // 2 * c)[None, :]).astype(BF) for c in (core, 1 - core)
    ]
    small = (near, distant, noise, noise_theirs, pick_near, pick_far)
    *partials, running = make_potential(place, small, chol_vectors, chol_theirs, n)

    def added(parts):
        total = parts[0].astype(F32)
        for p in parts[1:]:
            total = total + p.astype(F32)
        return total.astype(BF)

    moved = [along(partials[k], "y", k) for k in range(n)]
    over_y = added([after(moved[0], *tables)] + moved[1:])
    piece = added([along(over_y[m], "z", m) for m in range(n)])
    plane = jnp.stack(
        [
            lax.ppermute(
                piece,
                ("x", "z"),
                [(n * a + b, n * ((b - a) % n) + (b + k) % n) for a in range(n) for b in range(n)],
            )
            for k in range(n)
        ]
    )
    plane_theirs = other_core(plane)
    tables = tables + [other_core(t) for t in tables]
    running = make_cross(place, after(running, plane), tables, halves, n)
    plane = after(plane, running)
    chosen = parent[x * w_grp + y].reshape(1) // w_grp
    mine = make_taylor(place, chosen, got, plane, plane_theirs, n, count)
    spread = jnp.stack([along(mine, "y", k) for k in range(n)])
    new_walkers = join(place, spread, other_core(spread), n, n_occ)

    energy = running[:1]
    for axis in ("x", "z", "y"):
        energy = sum([along(energy, axis, k) for k in range(n)])
        if axis == "x":
            energy = energy + other_core(energy)
    n_all = n_vec * 2 * n * n
    energies = lax.dynamic_slice_in_dim(energy[0], w_grp * x, w_grp) / n_all
    return new_walkers.transpose(0, 2, 1), energies


def solution(mesh):
    finer = Mesh(mesh.devices.reshape(4, 4, 4, 2), ("x", "y", "z", "core"))
    chol = ("y", "z", "core")
    placed = (
        P("x", None, None),
        P(),
        P(chol, "x", None),
        P(chol, "x", None),
        P("x", chol),
        P(),
    )
    return jax.shard_map(
        shards,
        mesh=finer,
        in_specs=placed,
        out_specs=(P("x", None, None), P("x")),
        check_vma=False,
    )
```

```python
import functools

import jax
import jax.numpy as jnp
from jax import lax
from jax.experimental import pallas as pl
from jax.experimental.pallas import tpu as pltpu
from jax.sharding import Mesh, PartitionSpec as P

TERMS = 4
BF = jnp.bfloat16
F32 = jnp.float32
HIGH = lax.Precision.HIGHEST
VMEM_LIMIT = 56 * 1024 * 1024
SMEM = pl.BlockSpec(memory_space=pltpu.SMEM)
VMEM = pl.BlockSpec(memory_space=pltpu.VMEM)


def params(**more):
    return pltpu.CompilerParams(vmem_limit_bytes=VMEM_LIMIT, **more)


def taking(us):
    return pl.CostEstimate(flops=int(us * 1.15e9), bytes_accessed=1, transcendentals=0)


def mm(a, b, dims=((1,), (0,)), precision=None):
    return lax.dot_general(
        a, b, (dims, ((), ())), precision=precision, preferred_element_type=F32
    )


def shift(n, k):
    return [(q, (q + k) % n) for q in range(n)]


def theta_kernel(n, quarter, place, trial, walkers, *rest):
    own, (sent, c_ref, s_ref, y_ref, w_ref, h_ref, whole) = rest[:n], rest[n:]
    x_at, z_at, core = place[0], place[2], place[3]
    pair, rows = own[0].shape[:2]
    n_occ = trial.shape[0]
    ids = [lax.broadcasted_iota(jnp.int32, (n_occ, n_occ), d) for d in (0, 1)]
    eye = (ids[0] == ids[1]).astype(F32)
    for i in range(pair):
        w = walkers[pair * core + i]
        c = mm(trial[...], w, ((1,), (1,)))
        ct = mm(w, trial[...], ((1,), (1,)))
        c_ref[i] = ct
        g = jnp.abs(mm(c.astype(BF), ct.astype(BF)))
        side = jnp.max(jnp.sum(jnp.abs(c), axis=0)) * jnp.max(jnp.sum(jnp.abs(ct), axis=0))
        bound = jnp.max(jnp.sum(g, axis=0)) * 1.01 + side / 128.0
        start = c * (1.9 / jnp.full(ct.shape, bound, F32))
        s_ref[i] = start
        y_ref[i] = start

    def coarse(state):
        step, _ = state
        ys = [y_ref[i] for i in range(pair)]
        rs = [eye - mm(c_ref[i].astype(BF), ys[i].astype(BF)) for i in range(pair)]
        for i in range(pair):
            y_ref[i] = ys[i] + mm(ys[i].astype(BF), rs[i].astype(BF))
        return step + 1, sum(jnp.sum(r * r) for r in rs)

    def fine(state):
        step, _ = state
        ys = [y_ref[i] for i in range(pair)]
        rs = [eye - mm(c_ref[i], ys[i], precision=HIGH) for i in range(pair)]
        bs = [r.astype(BF) for r in rs]
        twos = [(rs[i] + mm(bs[i], bs[i])).astype(BF) for i in range(pair)]
        for i in range(pair):
            y_ref[i] = ys[i] + mm(ys[i].astype(BF), twos[i])
        return step + 1, sum(jnp.sum(r * r) for r in rs)

    def far(limit, tolerance):
        return lambda state: (state[0] < limit) & jnp.logical_not(state[1] < tolerance)

    begin = (jnp.int32(0), jnp.float32(1e30))
    lax.while_loop(far(14, 0.3), coarse, begin)
    _, left = lax.while_loop(far(6, 0.005), fine, begin)

    @pl.when(jnp.logical_not(left < 0.005))
    def _():
        y_ref[...] = s_ref[...]
        lax.while_loop(far(60, 0.005), fine, begin)

    for i in range(pair):
        inv = y_ref[i]
        high = inv.astype(BF)
        low = (inv - high.astype(F32)).astype(BF)
        w = walkers[pair * core + i]
        turned = mm(high, w) + mm(low, w)
        w_ref[i * n_occ : (i + 1) * n_occ, :] = turned
        h_ref[...] = turned.T.astype(BF)
        for j in range(n):
            block = lax.rem(x_at + j, n)
            own[j][i] = h_ref[pl.ds(pl.multiple_of(block * rows, rows), rows), :]
    whole[...] = w_ref[...].astype(BF)
    stride = (whole.shape[0] - quarter) // (n - 1)
    count = sent.shape[1] - quarter
    far = n_occ - count
    for j in range(n):
        sent[j, :quarter, :] = whole[pl.ds(pl.multiple_of(z_at * stride, stride), quarter), :]
        sent[j, quarter:, :] = walkers[jnp.clip(place[4 + j] - 2 * pair * x_at, 0, 2 * pair - 1), pl.ds(pl.multiple_of(core * far, far), count), :]


def make_theta(place, trial, walkers, n, quarter, count):
    _, n_occ, n_orb = walkers.shape
    pair = walkers.shape[0] // 2
    return pl.pallas_call(
        functools.partial(theta_kernel, n, quarter),
        out_shape=[jax.ShapeDtypeStruct((pair, n_orb // n, n_occ), BF)] * n
        + [
            jax.ShapeDtypeStruct((n, quarter + count, n_orb), BF),
        ],
        in_specs=[SMEM, VMEM, VMEM],
        out_specs=[VMEM] * (n + 1),
        scratch_shapes=[pltpu.VMEM((pair, n_occ, n_occ), F32)] * 3
        + [
            pltpu.VMEM((pair * n_occ, n_orb), F32),
            pltpu.VMEM((n_orb, n_occ), BF),
            pltpu.VMEM((pair * n_occ, n_orb), BF),
        ],
        compiler_params=params(),
        cost_estimate=taking(7.6),
        name="theta",
    )(place, trial, walkers)


def bias_kernel(n, place, mine, theirs, noise_mine, noise_theirs, *rest):
    thetas, (out, t_ref, acc) = rest[:n], rest[n:]
    x_at, core = place[0], place[3]
    pair, rows, n_occ = thetas[0].shape
    lanes = 32
    chunks = rows // lanes
    block = mine.shape[0]
    n_vec = acc.shape[1]
    walkers = out.shape[0]
    width = n * pair * lanes
    step = pl.program_id(0)
    sub = 8

    @pl.when(step == 0)
    def _():
        for k in range(n):
            for i in range(pair):
                at = (k * pair + i) * lanes
                t_ref[:, at : at + lanes, :] = thetas[k][i].reshape(chunks, lanes, n_occ)

    along = lax.broadcasted_iota(jnp.int32, (1, lanes // sub, sub, width), 3) % lanes
    row = sub * lax.broadcasted_iota(jnp.int32, along.shape, 1) + lax.broadcasted_iota(
        jnp.int32, along.shape, 2
    )
    for side, ref in enumerate((mine, theirs)):
        got = jnp.zeros((block * lanes, width), F32)
        for c in range(chunks):
            left = ref[:, c * lanes : (c + 1) * lanes, :].reshape(block * lanes, n_occ)
            got = got + mm(left, t_ref[c], ((1,), (1,)))
        got = got.reshape(block, lanes // sub, sub, width)
        kept = jnp.sum(jnp.where(along == row, got, 0.0), axis=1)
        acc[core if side == 0 else 1 - core, pl.ds(step * block, block)] = kept

    @pl.when(step == pl.num_programs(0) - 1)
    def _():
        lane = lax.broadcasted_iota(jnp.int32, (width, walkers), 0) // lanes
        column = lax.broadcasted_iota(jnp.int32, (width, walkers), 1)
        spot = pair * ((x_at - lane // pair + n) % n) + lane % pair
        sums = jnp.sum(acc[...].reshape(2 * n_vec, sub, width), axis=1)
        out[...] = -0.5 * mm((spot == column).astype(F32), sums, ((0,), (1,)), HIGH)
        own = pair_noise(place, noise_mine, noise_theirs, pair)
        row = lax.broadcasted_iota(jnp.int32, (walkers, pair), 0)
        which = lax.broadcasted_iota(jnp.int32, (walkers, pair), 1) + pair * x_at
        out[...] += mm((row == which).astype(F32), own, precision=HIGH)


def pair_noise(place, mine, theirs, pair):
    core = place[3]
    count, n_vec = mine.shape
    walker = lax.broadcasted_iota(jnp.int32, (pair, count), 1) - pair * core
    pick = (walker == lax.broadcasted_iota(jnp.int32, (pair, count), 0)).astype(F32)
    vec = lax.broadcasted_iota(jnp.int32, (n_vec, 2 * n_vec), 0)
    spot = lax.broadcasted_iota(jnp.int32, (n_vec, 2 * n_vec), 1)
    near = mm(mine[...], (vec + core * n_vec == spot).astype(F32), precision=HIGH)
    far = mm(theirs[...], (vec + (1 - core) * n_vec == spot).astype(F32), precision=HIGH)
    return mm(pick, near + far, precision=HIGH)


def make_bias(place, mine, theirs, noise_mine, noise_theirs, thetas, n):
    n_vec, rows, n_occ = mine.shape
    pair = thetas[0].shape[0]
    walkers = n * pair
    lanes = 32
    block = 14
    return pl.pallas_call(
        functools.partial(bias_kernel, n),
        out_shape=jax.ShapeDtypeStruct((walkers, 2 * n_vec), F32),
        grid=(n_vec // block,),
        in_specs=[SMEM]
        + [pl.BlockSpec((block, rows, n_occ), lambda s: (s, 0, 0))] * 2
        + [VMEM] * (2 + n),
        out_specs=VMEM,
        scratch_shapes=[
            pltpu.VMEM((rows // lanes, n * pair * lanes, n_occ), BF),
            pltpu.VMEM((2, n_vec, 8, n * pair * lanes), F32),
        ],
        compiler_params=params(),
        cost_estimate=taking(0.01),
        name="bias",
    )(place, mine, theirs, noise_mine, noise_theirs, *thetas)


def potential_kernel(n, place, near, far, noise_mine, noise_theirs, pick_near, pick_far, mine, theirs, *rest):
    outs = rest[:n]
    squares, a_ref = rest[n:]
    core = place[3]
    n_vec, lanes, n_orb = mine.shape
    x_at = place[0]
    slots = pick_near.shape[0]

    @pl.when(pl.program_id(0) == 0)
    def _():
        chosen = (
            mm(pick_near[...], near[...].astype(BF)) + mm(pick_far[...], far[...].astype(BF))
        ).astype(BF)
        pair = near.shape[0] // n
        row = lax.broadcasted_iota(jnp.int32, (pair, n * pair), 0) + pair * x_at
        which = lax.broadcasted_iota(jnp.int32, (pair, n * pair), 1)
        field = mm((row == which).astype(F32), near[...], precision=HIGH)
        bias = 2.0 * (pair_noise(place, noise_mine, noise_theirs, pair) - field)
        total = jnp.sum(bias * bias, axis=1, keepdims=True)
        lane = lax.broadcasted_iota(jnp.int32, (pair, slots), 1)
        walker = 2 * pair * x_at + pair * core + lax.broadcasted_iota(jnp.int32, (pair, slots), 0)
        spread = jnp.sum(jnp.where(lane == walker, 0.5 * total, 0.0), axis=0, keepdims=True)
        squares[...] = jnp.broadcast_to(spread, squares.shape)
        vec = lax.broadcasted_iota(jnp.int32, (n_vec, n_vec * lanes), 0)
        lane = lax.broadcasted_iota(jnp.int32, (n_vec, n_vec * lanes), 1)
        repeat = (lane // lanes == vec).astype(F32).astype(BF)
        sub = lax.broadcasted_iota(jnp.int32, (lanes, n_vec * lanes), 0)
        along = lax.broadcasted_iota(jnp.int32, (lanes, n_vec * lanes), 1) % lanes
        same = (sub == along).astype(F32)
        for c in range(2):
            wide = mm(chosen[:, c * n_vec : (c + 1) * n_vec], repeat)
            for s in range(slots):
                a_ref[c, s * lanes : (s + 1) * lanes, :] = (same * wide[s : s + 1, :]).astype(BF)

    got = mm(a_ref[core], mine[...].reshape(n_vec * lanes, n_orb)) + mm(
        a_ref[1 - core], theirs[...].reshape(n_vec * lanes, n_orb)
    )
    got = got.astype(BF).reshape(slots, lanes, n_orb)
    each = slots // n
    for k in range(n):
        outs[k][...] = got[k * each : (k + 1) * each]


def make_potential(place, small, mine, theirs, n):
    n_vec, rows, n_orb = mine.shape
    slots = small[-1].shape[0]
    half = rows // 2
    lanes = 16
    steps = half // lanes
    rows_of = pl.BlockSpec((n_vec, lanes, n_orb), lambda s, p: (0, p[3] * steps + s, 0))
    return pl.pallas_call(
        functools.partial(potential_kernel, n),
        out_shape=[jax.ShapeDtypeStruct((slots // n, half, n_orb), BF)] * n
        + [jax.ShapeDtypeStruct((8, slots), F32)],
        grid_spec=pltpu.PrefetchScalarGridSpec(
            num_scalar_prefetch=1,
            grid=(steps,),
            in_specs=[VMEM] * len(small) + [rows_of, rows_of],
            out_specs=[pl.BlockSpec((slots // n, lanes, n_orb), lambda s, p: (0, s, 0))] * n + [VMEM],
            scratch_shapes=[pltpu.VMEM((2, slots * lanes, n_vec * lanes), BF)],
        ),
        compiler_params=params(),
        cost_estimate=taking(0.01),
        name="potential",
    )(place, *small, mine, theirs)


def cross_kernel(n, pair, place, before, *rest):
    mine, theirs, halves = rest[:n], rest[n : 2 * n], rest[2 * n]
    out, t_ref, h_ref, p_ref, acc = rest[2 * n + 1 :]
    rows, n_occ = halves.shape[2:]
    z_at, core = place[2], place[3]
    block, count = pair * n_occ, mine[0].shape[1]
    stride = (block - count) // (n - 1)
    walkers = 2 * n * pair
    step = pl.program_id(0)

    @pl.when(step == 0)
    def _():
        acc[...] = jnp.zeros(acc.shape, F32)
        p_ref[...] = jnp.zeros(p_ref.shape, BF)
        for c, tables in enumerate((mine, theirs)):
            for j in range(n):
                start = stride * lax.rem(z_at - j + n, n)
                for k in range(n):
                    at = pl.multiple_of((c * n + k) * block + start, 16)
                    t_ref[pl.ds(at, count), :] = tables[j][k]

    def square():
        for w in range(walkers):
            p = p_ref[w]
            acc[w] += mm(p, p)

    for s in range(n):
        h_ref[s * rows : (s + 1) * rows, :] = halves[s, 0]
    square()
    for q in range(2 * n):
        got = mm(t_ref[q * block : (q + 1) * block, :], h_ref[...])
        for i in range(pair):
            p_ref[q * pair + i] = got[i * n_occ : (i + 1) * n_occ].astype(BF)

    @pl.when(step == pl.num_programs(0) - 1)
    def _():
        square()
        ids = [lax.broadcasted_iota(jnp.int32, (n_occ, n_occ), d) for d in (0, 1)]
        lane = lax.broadcasted_iota(jnp.int32, out.shape, 1)
        total = before[...]
        for c in range(2):
            for k in range(n):
                for i in range(pair):
                    got = acc[(c * n + k) * pair + i]
                    value = jnp.sum(jnp.where(ids[0] == ids[1], got, 0.0))
                    parity = core if c == 0 else 1 - core
                    walker = 2 * pair * k + pair * parity + i
                    total = total + jnp.where(lane == walker, -0.5 * value, 0.0)
        out[...] = total


def make_cross(place, before, tables, halves, n):
    _, steps, rows, n_occ = halves.shape
    n_orb = tables[0].shape[2]
    pair = 2
    walkers = 2 * n * pair
    return pl.pallas_call(
        functools.partial(cross_kernel, n, pair),
        out_shape=jax.ShapeDtypeStruct(before.shape, F32),
        grid=(steps,),
        in_specs=[SMEM]
        + [VMEM] * (2 * n + 1)
        + [pl.BlockSpec((n, 1, rows, n_occ), lambda s: (0, s, 0, 0))],
        out_specs=VMEM,
        scratch_shapes=[
            pltpu.VMEM((walkers * n_occ, n_orb), BF),
            pltpu.VMEM((n_orb, n_occ), BF),
            pltpu.VMEM((walkers, n_occ, n_occ), BF),
            pltpu.VMEM((walkers, n_occ, n_occ), F32),
        ],
        compiler_params=params(),
        cost_estimate=taking(0.5),
        name="cross",
    )(place, before, *tables, halves)


def taylor_kernel(n, place, walker, mine, theirs, out, v_ref):
    x_at, z_at, core = place[0], place[2], place[3]
    half = mine.shape[1]
    for k in range(n):
        block = lax.rem(z_at - k - x_at + 2 * n, n)
        v_ref[pl.ds(pl.multiple_of((2 * block + core) * half, half), half), :] = mine[k]
        v_ref[pl.ds(pl.multiple_of((2 * block + 1 - core) * half, half), half), :] = theirs[k]

    term = walker[lax.div(place[4 + x_at], n), walker.shape[1] - out.shape[0] :, :]
    total = term.astype(F32)
    for k in range(1, TERMS + 1):
        term = (mm(term, v_ref[...], ((1,), (1,))) / k).astype(BF)
        total = total + term.astype(F32)
    out[...] = total.astype(BF)


def make_taylor(place, walkers, mine, theirs, n, count):
    n_orb = walkers.shape[2]
    return pl.pallas_call(
        functools.partial(taylor_kernel, n),
        out_shape=jax.ShapeDtypeStruct((count, n_orb), BF),
        in_specs=[SMEM] + [VMEM] * 3,
        out_specs=VMEM,
        scratch_shapes=[pltpu.VMEM((n_orb, n_orb), BF)],
        compiler_params=params(),
        cost_estimate=taking(0.01),
        name="taylor",
    )(place, walkers, mine, theirs)


def join_kernel(n, place, mine, theirs, out):
    y_at, core = place[1], place[3]
    count = mine.shape[1]
    far = out.shape[1] - count
    for k in range(n):
        slot = lax.rem(y_at - k + n, n)
        out[slot, pl.ds(pl.multiple_of(core * far, far), count), :] = mine[k]
        out[slot, pl.ds(pl.multiple_of((1 - core) * far, far), count), :] = theirs[k]


def join(place, mine, theirs, n, n_occ):
    n_orb = mine.shape[2]
    return pl.pallas_call(
        functools.partial(join_kernel, n),
        out_shape=jax.ShapeDtypeStruct((n, n_occ, n_orb), BF),
        in_specs=[SMEM, VMEM, VMEM],
        out_specs=VMEM,
        compiler_params=params(),
        cost_estimate=taking(0.01),
        name="join",
    )(place, mine, theirs)


def after(value, *earlier):
    return lax.optimization_barrier((value, *earlier))[0]


def shards(walkers, trial, half_chol, chol_vectors, noise, copies):
    n = lax.axis_size("x")
    x, y, z, core = (lax.axis_index(a) for a in ("x", "y", "z", "core"))
    w_grp, n_orb, n_occ = walkers.shape
    n_vec = half_chol.shape[0]
    slots = w_grp * n
    walkers = walkers.transpose(0, 2, 1)
    trial = trial.T
    other_core = functools.partial(lax.ppermute, axis_name="core", perm=[(0, 1), (1, 0)])

    def along(v, axis, k):
        return lax.ppermute(v, axis, shift(n, k)) if k else v

    numbers = jnp.arange(slots, dtype=jnp.int32)
    ends = jnp.sum(jnp.where(numbers[None, :] <= numbers[:, None], copies[None, :], 0), axis=1)
    parent = jnp.sum(
        (ends[None, :] <= numbers[:, None]).astype(jnp.int32),
        axis=1,
    )

    noise_theirs = other_core(noise)
    half_theirs = other_core(half_chol)
    quarter, count = 112, 104
    wanted = jnp.sum(jnp.where(jnp.arange(w_grp) == y, parent.reshape(n, w_grp), 0), axis=1)
    place = jnp.concatenate([jnp.stack([x, y, z, core]), wanted]).astype(jnp.int32)
    *own, sent = make_theta(place, trial, walkers, n, quarter, count)
    own = [own[0]] + [after(t, half_theirs, noise_theirs) for t in own[1:]]
    thetas = [along(own[k], "x", k) for k in range(n)]
    got = lax.all_to_all(after(sent, *thetas[1:]), "x", 0, 0, tiled=True)
    chol_theirs = other_core(after(chol_vectors, own[0], half_theirs, noise_theirs))

    share = make_bias(place, half_chol, half_theirs, noise, noise_theirs, thetas, n)
    near = lax.psum(share, "x")
    got = after(got, near)
    distant = other_core(near)
    by_x = half_chol.reshape((n, n_vec // n) + half_chol.shape[1:])
    halves = lax.all_to_all(after(by_x, near), "x", 0, 0, tiled=True)

    order = jnp.array([[k, m] for k in range(n) for m in range(n)], jnp.int32)
    slot = w_grp * ((z + order[:, 1] - x) % n) + (y + order[:, 0]) % n
    pairs = jnp.array([w_grp * a + i for a in range(n) for i in range(w_grp // 2)], jnp.int32)
    pick_near, pick_far = [
        (parent[slot][:, None] == (pairs + w_grp // 2 * c)[None, :]).astype(BF) for c in (core, 1 - core)
    ]
    small = (near, distant, noise, noise_theirs, pick_near, pick_far)
    *partials, running = make_potential(place, small, chol_vectors, chol_theirs, n)

    def added(parts):
        total = parts[0].astype(F32)
        for p in parts[1:]:
            total = total + p.astype(F32)
        return total.astype(BF)

    pieces = after(got[:, :quarter], partials[0])
    after_one, before_one = along(pieces, "z", 1), along(pieces, "z", 3)
    opposite = jnp.concatenate(
        [along(after_one[: n // 2], "z", 1), along(before_one[n // 2 :], "z", 3)], axis=0
    )
    tables = [pieces, after_one, opposite, before_one]
    over_y = added([along(partials[k], "y", k) for k in range(n)])
    piece = added([along(over_y[m], "z", m) for m in range(n)])
    plane = jnp.stack(
        [
            lax.ppermute(
                piece,
                ("x", "z"),
                [(n * a + b, n * ((b - a) % n) + (b + k) % n) for a in range(n) for b in range(n)],
            )
            for k in range(n)
        ]
    )
    plane_theirs = other_core(plane)
    tables = tables + [other_core(t) for t in tables]
    running = make_cross(place, after(running, plane), tables, halves, n)
    plane = after(plane, running)
    energy = running[:1]
    over_x = [along(energy, "x", k) for k in range(n)]
    mine = make_taylor(after(place, over_x[1]), got, plane, plane_theirs, n, count)
    spread = jnp.stack([along(mine, "y", k) for k in range(n)])
    new_walkers = join(place, spread, other_core(spread), n, n_occ)

    energy = sum(over_x)
    energy = energy + other_core(energy)
    for axis in ("z", "y"):
        energy = sum([along(energy, axis, k) for k in range(n)])
    n_all = n_vec * 2 * n * n
    energies = lax.dynamic_slice_in_dim(energy[0], w_grp * x, w_grp) / n_all
    return new_walkers.transpose(0, 2, 1), energies


def solution(mesh):
    finer = Mesh(mesh.devices.reshape(4, 4, 4, 2), ("x", "y", "z", "core"))
    chol = ("y", "z", "core")
    placed = (
        P("x", None, None),
        P(),
        P(chol, "x", None),
        P(chol, "x", None),
        P("x", chol),
        P(),
    )
    return jax.shard_map(
        shards,
        mesh=finer,
        in_specs=placed,
        out_specs=(P("x", None, None), P("x")),
        check_vma=False,
    )
```

```python
import functools

import jax
import jax.numpy as jnp
from jax import lax
from jax.experimental import pallas as pl
from jax.experimental.pallas import tpu as pltpu
from jax.sharding import Mesh, PartitionSpec as P

TERMS = 4
BF = jnp.bfloat16
F32 = jnp.float32
HIGH = lax.Precision.HIGHEST
VMEM_LIMIT = 56 * 1024 * 1024
SMEM = pl.BlockSpec(memory_space=pltpu.SMEM)
VMEM = pl.BlockSpec(memory_space=pltpu.VMEM)


def params(**more):
    return pltpu.CompilerParams(vmem_limit_bytes=VMEM_LIMIT, **more)


def taking(us):
    return pl.CostEstimate(flops=int(us * 1.15e9), bytes_accessed=1, transcendentals=0)


def mm(a, b, dims=((1,), (0,)), precision=None):
    return lax.dot_general(
        a, b, (dims, ((), ())), precision=precision, preferred_element_type=F32
    )


def shift(n, k):
    return [(q, (q + k) % n) for q in range(n)]


def theta_kernel(n, quarter, place, trial, walkers, *rest):
    own, (sent, c_ref, s_ref, y_ref, w_ref, h_ref, whole) = rest[:n], rest[n:]
    x_at, z_at, core = place[0], place[2], place[3]
    pair, rows = own[0].shape[:2]
    n_occ = trial.shape[0]
    ids = [lax.broadcasted_iota(jnp.int32, (n_occ, n_occ), d) for d in (0, 1)]
    eye = (ids[0] == ids[1]).astype(F32)
    for i in range(pair):
        w = walkers[pair * core + i]
        c = mm(trial[...], w, ((1,), (1,)))
        ct = mm(w, trial[...], ((1,), (1,)))
        c_ref[i] = ct
        g = jnp.abs(mm(c.astype(BF), ct.astype(BF)))
        side = jnp.max(jnp.sum(jnp.abs(c), axis=0)) * jnp.max(jnp.sum(jnp.abs(ct), axis=0))
        bound = jnp.max(jnp.sum(g, axis=0)) * 1.01 + side / 128.0
        start = c * (1.9 / jnp.full(ct.shape, bound, F32))
        s_ref[i] = start
        y_ref[i] = start

    def coarse(state):
        step, _ = state
        ys = [y_ref[i] for i in range(pair)]
        rs = [eye - mm(c_ref[i].astype(BF), ys[i].astype(BF)) for i in range(pair)]
        for i in range(pair):
            y_ref[i] = ys[i] + mm(ys[i].astype(BF), rs[i].astype(BF))
        return step + 1, sum(jnp.sum(r * r) for r in rs)

    def fine(state):
        step, _ = state
        ys = [y_ref[i] for i in range(pair)]
        rs = [eye - mm(c_ref[i], ys[i], precision=HIGH) for i in range(pair)]
        bs = [r.astype(BF) for r in rs]
        twos = [(rs[i] + mm(bs[i], bs[i])).astype(BF) for i in range(pair)]
        for i in range(pair):
            y_ref[i] = ys[i] + mm(ys[i].astype(BF), twos[i])
        return step + 1, sum(jnp.sum(r * r) for r in rs)

    def far(limit, tolerance):
        return lambda state: (state[0] < limit) & jnp.logical_not(state[1] < tolerance)

    begin = (jnp.int32(0), jnp.float32(1e30))
    lax.while_loop(far(14, 0.3), coarse, begin)
    _, left = lax.while_loop(far(6, 0.005), fine, begin)

    @pl.when(jnp.logical_not(left < 0.005))
    def _():
        y_ref[...] = s_ref[...]
        lax.while_loop(far(60, 0.005), fine, begin)

    for i in range(pair):
        inv = y_ref[i]
        high = inv.astype(BF)
        low = (inv - high.astype(F32)).astype(BF)
        w = walkers[pair * core + i]
        turned = mm(high, w) + mm(low, w)
        w_ref[i * n_occ : (i + 1) * n_occ, :] = turned
        h_ref[...] = turned.T.astype(BF)
        for j in range(n):
            block = lax.rem(x_at + j, n)
            own[j][i] = h_ref[pl.ds(pl.multiple_of(block * rows, rows), rows), :]
    whole[...] = w_ref[...].astype(BF)
    stride = (whole.shape[0] - quarter) // (n - 1)
    count = sent.shape[1] - quarter
    far = n_occ - count
    for j in range(n):
        sent[j, :quarter, :] = whole[pl.ds(pl.multiple_of(z_at * stride, stride), quarter), :]
        sent[j, quarter:, :] = walkers[jnp.clip(place[4 + j] - 2 * pair * x_at, 0, 2 * pair - 1), pl.ds(pl.multiple_of(core * far, far), count), :]


def make_theta(place, trial, walkers, n, quarter, count):
    _, n_occ, n_orb = walkers.shape
    pair = walkers.shape[0] // 2
    return pl.pallas_call(
        functools.partial(theta_kernel, n, quarter),
        out_shape=[jax.ShapeDtypeStruct((pair, n_orb // n, n_occ), BF)] * n
        + [
            jax.ShapeDtypeStruct((n, quarter + count, n_orb), BF),
        ],
        in_specs=[SMEM, VMEM, VMEM],
        out_specs=[VMEM] * (n + 1),
        scratch_shapes=[pltpu.VMEM((pair, n_occ, n_occ), F32)] * 3
        + [
            pltpu.VMEM((pair * n_occ, n_orb), F32),
            pltpu.VMEM((n_orb, n_occ), BF),
            pltpu.VMEM((pair * n_occ, n_orb), BF),
        ],
        compiler_params=params(),
        cost_estimate=taking(7.6),
        name="theta",
    )(place, trial, walkers)


def bias_kernel(n, place, mine, theirs, noise_mine, noise_theirs, *rest):
    thetas, (out, t_ref, acc) = rest[:n], rest[n:]
    x_at, core = place[0], place[3]
    pair, rows, n_occ = thetas[0].shape
    lanes = 32
    chunks = rows // lanes
    block = mine.shape[0]
    n_vec = acc.shape[1]
    walkers = out.shape[0]
    width = n * pair * lanes
    step = pl.program_id(0)
    sub = 8

    @pl.when(step == 0)
    def _():
        for k in range(n):
            for i in range(pair):
                at = (k * pair + i) * lanes
                t_ref[:, at : at + lanes, :] = thetas[k][i].reshape(chunks, lanes, n_occ)

    along = lax.broadcasted_iota(jnp.int32, (1, lanes // sub, sub, width), 3) % lanes
    row = sub * lax.broadcasted_iota(jnp.int32, along.shape, 1) + lax.broadcasted_iota(
        jnp.int32, along.shape, 2
    )
    for side, ref in enumerate((mine, theirs)):
        got = jnp.zeros((block * lanes, width), F32)
        for c in range(chunks):
            left = ref[:, c * lanes : (c + 1) * lanes, :].reshape(block * lanes, n_occ)
            got = got + mm(left, t_ref[c], ((1,), (1,)))
        got = got.reshape(block, lanes // sub, sub, width)
        kept = jnp.sum(jnp.where(along == row, got, 0.0), axis=1)
        acc[core if side == 0 else 1 - core, pl.ds(step * block, block)] = kept

    @pl.when(step == pl.num_programs(0) - 1)
    def _():
        lane = lax.broadcasted_iota(jnp.int32, (width, walkers), 0) // lanes
        column = lax.broadcasted_iota(jnp.int32, (width, walkers), 1)
        spot = pair * ((x_at - lane // pair + n) % n) + lane % pair
        sums = jnp.sum(acc[...].reshape(2 * n_vec, sub, width), axis=1)
        out[...] = -0.5 * mm((spot == column).astype(F32), sums, ((0,), (1,)), HIGH)
        own = pair_noise(place, noise_mine, noise_theirs, pair)
        row = lax.broadcasted_iota(jnp.int32, (walkers, pair), 0)
        which = lax.broadcasted_iota(jnp.int32, (walkers, pair), 1) + pair * x_at
        out[...] += mm((row == which).astype(F32), own, precision=HIGH)


def pair_noise(place, mine, theirs, pair):
    core = place[3]
    count, n_vec = mine.shape
    walker = lax.broadcasted_iota(jnp.int32, (pair, count), 1) - pair * core
    pick = (walker == lax.broadcasted_iota(jnp.int32, (pair, count), 0)).astype(F32)
    vec = lax.broadcasted_iota(jnp.int32, (n_vec, 2 * n_vec), 0)
    spot = lax.broadcasted_iota(jnp.int32, (n_vec, 2 * n_vec), 1)
    near = mm(mine[...], (vec + core * n_vec == spot).astype(F32), precision=HIGH)
    far = mm(theirs[...], (vec + (1 - core) * n_vec == spot).astype(F32), precision=HIGH)
    return mm(pick, near + far, precision=HIGH)


def make_bias(place, mine, theirs, noise_mine, noise_theirs, thetas, n):
    n_vec, rows, n_occ = mine.shape
    pair = thetas[0].shape[0]
    walkers = n * pair
    lanes = 32
    block = 28
    return pl.pallas_call(
        functools.partial(bias_kernel, n),
        out_shape=jax.ShapeDtypeStruct((walkers, 2 * n_vec), F32),
        grid=(n_vec // block,),
        in_specs=[SMEM]
        + [pl.BlockSpec((block, rows, n_occ), lambda s: (s, 0, 0))] * 2
        + [VMEM] * (2 + n),
        out_specs=VMEM,
        scratch_shapes=[
            pltpu.VMEM((rows // lanes, n * pair * lanes, n_occ), BF),
            pltpu.VMEM((2, n_vec, 8, n * pair * lanes), F32),
        ],
        compiler_params=params(),
        cost_estimate=taking(0.01),
        name="bias",
    )(place, mine, theirs, noise_mine, noise_theirs, *thetas)


def potential_kernel(n, place, near, far, noise_mine, noise_theirs, pick_near, pick_far, mine, theirs, *rest):
    outs = rest[:n]
    squares, a_ref = rest[n:]
    core = place[3]
    n_vec, lanes, n_orb = mine.shape
    x_at = place[0]
    slots = pick_near.shape[0]

    @pl.when(pl.program_id(0) == 0)
    def _():
        chosen = (
            mm(pick_near[...], near[...].astype(BF)) + mm(pick_far[...], far[...].astype(BF))
        ).astype(BF)
        pair = near.shape[0] // n
        row = lax.broadcasted_iota(jnp.int32, (pair, n * pair), 0) + pair * x_at
        which = lax.broadcasted_iota(jnp.int32, (pair, n * pair), 1)
        field = mm((row == which).astype(F32), near[...], precision=HIGH)
        bias = 2.0 * (pair_noise(place, noise_mine, noise_theirs, pair) - field)
        total = jnp.sum(bias * bias, axis=1, keepdims=True)
        lane = lax.broadcasted_iota(jnp.int32, (pair, slots), 1)
        walker = 2 * pair * x_at + pair * core + lax.broadcasted_iota(jnp.int32, (pair, slots), 0)
        spread = jnp.sum(jnp.where(lane == walker, 0.5 * total, 0.0), axis=0, keepdims=True)
        squares[...] = jnp.broadcast_to(spread, squares.shape)
        vec = lax.broadcasted_iota(jnp.int32, (n_vec, n_vec * lanes), 0)
        lane = lax.broadcasted_iota(jnp.int32, (n_vec, n_vec * lanes), 1)
        repeat = (lane // lanes == vec).astype(F32).astype(BF)
        sub = lax.broadcasted_iota(jnp.int32, (lanes, n_vec * lanes), 0)
        along = lax.broadcasted_iota(jnp.int32, (lanes, n_vec * lanes), 1) % lanes
        same = (sub == along).astype(F32)
        for c in range(2):
            wide = mm(chosen[:, c * n_vec : (c + 1) * n_vec], repeat)
            for s in range(slots):
                a_ref[c, s * lanes : (s + 1) * lanes, :] = (same * wide[s : s + 1, :]).astype(BF)

    got = mm(a_ref[core], mine[...].reshape(n_vec * lanes, n_orb)) + mm(
        a_ref[1 - core], theirs[...].reshape(n_vec * lanes, n_orb)
    )
    got = got.astype(BF).reshape(slots, lanes, n_orb)
    each = slots // n
    for k in range(n):
        outs[k][...] = got[k * each : (k + 1) * each]


def make_potential(place, small, mine, theirs, n):
    n_vec, rows, n_orb = mine.shape
    slots = small[-1].shape[0]
    half = rows // 2
    lanes = 16
    steps = half // lanes
    rows_of = pl.BlockSpec((n_vec, lanes, n_orb), lambda s, p: (0, p[3] * steps + s, 0))
    return pl.pallas_call(
        functools.partial(potential_kernel, n),
        out_shape=[jax.ShapeDtypeStruct((slots // n, half, n_orb), BF)] * n
        + [jax.ShapeDtypeStruct((8, slots), F32)],
        grid_spec=pltpu.PrefetchScalarGridSpec(
            num_scalar_prefetch=1,
            grid=(steps,),
            in_specs=[VMEM] * len(small) + [rows_of, rows_of],
            out_specs=[pl.BlockSpec((slots // n, lanes, n_orb), lambda s, p: (0, s, 0))] * n + [VMEM],
            scratch_shapes=[pltpu.VMEM((2, slots * lanes, n_vec * lanes), BF)],
        ),
        compiler_params=params(),
        cost_estimate=taking(0.01),
        name="potential",
    )(place, *small, mine, theirs)


def cross_kernel(n, pair, place, before, *rest):
    mine, theirs, halves = rest[:n], rest[n : 2 * n], rest[2 * n]
    out, t_ref, h_ref, p_ref, acc = rest[2 * n + 1 :]
    rows, n_occ = halves.shape[2:]
    z_at, core = place[2], place[3]
    block, count = pair * n_occ, mine[0].shape[1]
    stride = (block - count) // (n - 1)
    walkers = 2 * n * pair
    step = pl.program_id(0)

    @pl.when(step == 0)
    def _():
        acc[...] = jnp.zeros(acc.shape, F32)
        p_ref[...] = jnp.zeros(p_ref.shape, BF)
        for c, tables in enumerate((mine, theirs)):
            for j in range(n):
                start = stride * lax.rem(z_at - j + n, n)
                for k in range(n):
                    at = pl.multiple_of((c * n + k) * block + start, 16)
                    t_ref[pl.ds(at, count), :] = tables[j][k]

    def square():
        for w in range(walkers):
            p = p_ref[w]
            acc[w] += mm(p, p)

    for s in range(n):
        h_ref[s * rows : (s + 1) * rows, :] = halves[s, 0]
    square()
    for q in range(2 * n):
        got = mm(t_ref[q * block : (q + 1) * block, :], h_ref[...])
        for i in range(pair):
            p_ref[q * pair + i] = got[i * n_occ : (i + 1) * n_occ].astype(BF)

    @pl.when(step == pl.num_programs(0) - 1)
    def _():
        square()
        ids = [lax.broadcasted_iota(jnp.int32, (n_occ, n_occ), d) for d in (0, 1)]
        lane = lax.broadcasted_iota(jnp.int32, out.shape, 1)
        total = before[...]
        for c in range(2):
            for k in range(n):
                for i in range(pair):
                    got = acc[(c * n + k) * pair + i]
                    value = jnp.sum(jnp.where(ids[0] == ids[1], got, 0.0))
                    parity = core if c == 0 else 1 - core
                    walker = 2 * pair * k + pair * parity + i
                    total = total + jnp.where(lane == walker, -0.5 * value, 0.0)
        out[...] = total


def make_cross(place, before, tables, halves, n):
    _, steps, rows, n_occ = halves.shape
    n_orb = tables[0].shape[2]
    pair = 2
    walkers = 2 * n * pair
    return pl.pallas_call(
        functools.partial(cross_kernel, n, pair),
        out_shape=jax.ShapeDtypeStruct(before.shape, F32),
        grid=(steps,),
        in_specs=[SMEM]
        + [VMEM] * (2 * n + 1)
        + [pl.BlockSpec((n, 1, rows, n_occ), lambda s: (0, s, 0, 0))],
        out_specs=VMEM,
        scratch_shapes=[
            pltpu.VMEM((walkers * n_occ, n_orb), BF),
            pltpu.VMEM((n_orb, n_occ), BF),
            pltpu.VMEM((walkers, n_occ, n_occ), BF),
            pltpu.VMEM((walkers, n_occ, n_occ), F32),
        ],
        compiler_params=params(),
        cost_estimate=taking(0.5),
        name="cross",
    )(place, before, *tables, halves)


def taylor_kernel(n, place, walker, mine, theirs, out, v_ref):
    x_at, z_at, core = place[0], place[2], place[3]
    half = mine.shape[1]
    for k in range(n):
        block = lax.rem(z_at - k - x_at + 2 * n, n)
        v_ref[pl.ds(pl.multiple_of((2 * block + core) * half, half), half), :] = mine[k]
        v_ref[pl.ds(pl.multiple_of((2 * block + 1 - core) * half, half), half), :] = theirs[k]

    term = walker[lax.div(place[4 + x_at], n), walker.shape[1] - out.shape[0] :, :]
    total = term.astype(F32)
    for k in range(1, TERMS + 1):
        term = (mm(term, v_ref[...], ((1,), (1,))) / k).astype(BF)
        total = total + term.astype(F32)
    out[...] = total.astype(BF)


def make_taylor(place, walkers, mine, theirs, n, count):
    n_orb = walkers.shape[2]
    return pl.pallas_call(
        functools.partial(taylor_kernel, n),
        out_shape=jax.ShapeDtypeStruct((count, n_orb), BF),
        in_specs=[SMEM] + [VMEM] * 3,
        out_specs=VMEM,
        scratch_shapes=[pltpu.VMEM((n_orb, n_orb), BF)],
        compiler_params=params(),
        cost_estimate=taking(0.01),
        name="taylor",
    )(place, walkers, mine, theirs)


def join_kernel(n, place, mine, theirs, out):
    y_at, core = place[1], place[3]
    count = mine.shape[1]
    far = out.shape[1] - count
    for k in range(n):
        slot = lax.rem(y_at - k + n, n)
        out[slot, pl.ds(pl.multiple_of(core * far, far), count), :] = mine[k]
        out[slot, pl.ds(pl.multiple_of((1 - core) * far, far), count), :] = theirs[k]


def join(place, mine, theirs, n, n_occ):
    n_orb = mine.shape[2]
    return pl.pallas_call(
        functools.partial(join_kernel, n),
        out_shape=jax.ShapeDtypeStruct((n, n_occ, n_orb), BF),
        in_specs=[SMEM, VMEM, VMEM],
        out_specs=VMEM,
        compiler_params=params(),
        cost_estimate=taking(0.01),
        name="join",
    )(place, mine, theirs)


def after(value, *earlier):
    return lax.optimization_barrier((value, *earlier))[0]


def shards(walkers, trial, half_chol, chol_vectors, noise, copies):
    n = lax.axis_size("x")
    x, y, z, core = (lax.axis_index(a) for a in ("x", "y", "z", "core"))
    w_grp, n_orb, n_occ = walkers.shape
    n_vec = half_chol.shape[0]
    slots = w_grp * n
    walkers = walkers.transpose(0, 2, 1)
    trial = trial.T
    other_core = functools.partial(lax.ppermute, axis_name="core", perm=[(0, 1), (1, 0)])

    def along(v, axis, k):
        return lax.ppermute(v, axis, shift(n, k)) if k else v

    numbers = jnp.arange(slots, dtype=jnp.int32)
    ends = jnp.sum(jnp.where(numbers[None, :] <= numbers[:, None], copies[None, :], 0), axis=1)
    parent = jnp.sum(
        (ends[None, :] <= numbers[:, None]).astype(jnp.int32),
        axis=1,
    )

    noise_theirs = other_core(noise)
    half_theirs = other_core(half_chol)
    quarter, count = 112, 104
    wanted = jnp.sum(jnp.where(jnp.arange(w_grp) == y, parent.reshape(n, w_grp), 0), axis=1)
    place = jnp.concatenate([jnp.stack([x, y, z, core]), wanted]).astype(jnp.int32)
    *own, sent = make_theta(place, trial, walkers, n, quarter, count)
    own = [own[0]] + [after(t, half_theirs, noise_theirs) for t in own[1:]]
    thetas = [along(own[k], "x", k) for k in range(n)]
    got = lax.all_to_all(after(sent, *thetas[1:]), "x", 0, 0, tiled=True)
    chol_theirs = other_core(after(chol_vectors, own[0], half_theirs, noise_theirs))

    share = make_bias(place, half_chol, half_theirs, noise, noise_theirs, thetas, n)
    near = lax.psum(share, "x")
    got = after(got, near)
    distant = other_core(near)
    by_x = half_chol.reshape((n, n_vec // n) + half_chol.shape[1:])
    halves = lax.all_to_all(after(by_x, near), "x", 0, 0, tiled=True)

    order = jnp.array([[k, m] for k in range(n) for m in range(n)], jnp.int32)
    slot = w_grp * ((z + order[:, 1] - x) % n) + (y + order[:, 0]) % n
    pairs = jnp.array([w_grp * a + i for a in range(n) for i in range(w_grp // 2)], jnp.int32)
    pick_near, pick_far = [
        (parent[slot][:, None] == (pairs + w_grp // 2 * c)[None, :]).astype(BF) for c in (core, 1 - core)
    ]
    small = (near, distant, noise, noise_theirs, pick_near, pick_far)
    *partials, running = make_potential(place, small, chol_vectors, chol_theirs, n)

    def added(parts):
        total = parts[0].astype(F32)
        for p in parts[1:]:
            total = total + p.astype(F32)
        return total.astype(BF)

    pieces = after(got[:, :quarter], partials[0])
    after_one, before_one = along(pieces, "z", 1), along(pieces, "z", 3)
    opposite = jnp.concatenate(
        [along(after_one[: n // 2], "z", 1), along(before_one[n // 2 :], "z", 3)], axis=0
    )
    tables = [pieces, after_one, opposite, before_one]
    over_y = added([along(partials[k], "y", k) for k in range(n)])
    piece = added([along(over_y[m], "z", m) for m in range(n)])
    plane = jnp.stack(
        [
            lax.ppermute(
                piece,
                ("x", "z"),
                [(n * a + b, n * ((b - a) % n) + (b + k) % n) for a in range(n) for b in range(n)],
            )
            for k in range(n)
        ]
    )
    plane_theirs = other_core(plane)
    tables = tables + [other_core(t) for t in tables]
    running = make_cross(place, after(running, plane), tables, halves, n)
    plane = after(plane, running)
    energy = running[:1]
    over_x = [along(energy, "x", k) for k in range(n)]
    mine = make_taylor(after(place, over_x[1]), got, plane, plane_theirs, n, count)
    spread = jnp.stack([along(mine, "y", k) for k in range(n)])
    new_walkers = join(place, spread, other_core(spread), n, n_occ)

    energy = sum(over_x)
    energy = energy + other_core(energy)
    for axis in ("z", "y"):
        energy = sum([along(energy, axis, k) for k in range(n)])
    n_all = n_vec * 2 * n * n
    energies = lax.dynamic_slice_in_dim(energy[0], w_grp * x, w_grp) / n_all
    return new_walkers.transpose(0, 2, 1), energies


def solution(mesh):
    finer = Mesh(mesh.devices.reshape(4, 4, 4, 2), ("x", "y", "z", "core"))
    chol = ("y", "z", "core")
    placed = (
        P("x", None, None),
        P(),
        P(chol, "x", None),
        P(chol, "x", None),
        P("x", chol),
        P(),
    )
    return jax.shard_map(
        shards,
        mesh=finer,
        in_specs=placed,
        out_specs=(P("x", None, None), P("x")),
        check_vma=False,
    )
```
